512 devices in a mesh: row: 32 (over z_lo, x, core), col: 16 (over y, z_hi).
Axes of the slice: x: 4, y: 4, z: 16 (z_hi: 4, z_lo: 4; z = z_hi * 4 + z_lo), core: 2. Of those that a mesh axis runs over, the one named last changes fastest.
Arguments:
- acts: bfloat16 [2048, 16384], P('row', 'col'), may hold values from -6 to 6
- grads: float32 [16384, 512], P('col', 'row'), may hold values from -24 to 24
Outputs:
- factor: float32 [16384, 16384], P('row', 'col')
- applied: float32 [16384, 512], P('row', 'col')
- solution: float32 [16384, 512], P('col', 'row')
The draws below stay inside these ranges and needn't reach their ends.
All inputs are finite; a program needn't handle non-finite values.
Results may differ from the reference program's by a relative error of at most 0.0003.
Values may be sent and summed in bfloat16 or wider, within the bound.
A program may use at most 64 MiB of HBM per device.

```python
import math
import jax
import jax.numpy as jnp
from jax import lax

D = 16384
NRHS = 512
TOKENS = 2048


def steps_of(own_key, extent, pieces, least, largest):
    factor_of, own = 1.0, jax.random.fold_in(own_key, 6)
    for dim, blocks in pieces:
        draws = jnp.exp(jax.random.uniform(jax.random.fold_in(own, dim), (blocks,), jnp.float32, least / len(pieces), largest / len(pieces)))
        factor_of = factor_of * jnp.repeat(draws, extent[dim] // blocks).reshape([-1 if axis == dim else 1 for axis in range(len(extent))])
    return factor_of


def scatter_about(own_key, extent, scale, bound, shards=(), held_as=jnp.bfloat16):
    factor_of = steps_of(own_key, extent, shards, -0.22, 0.18) if shards else 1.0
    entries = jax.random.normal(own_key, extent, jnp.float32) * scale * factor_of
    return jnp.minimum(jnp.maximum(entries, -bound), bound).astype(held_as)


def setup_inputs(seed: int = 0) -> dict:
    key_of = jax.random.split(jax.random.key(seed), 3)
    acts = scatter_about(key_of[0], (TOKENS, D), 1.0, 6.0, ((0, 32), (1, 16)))
    grads = scatter_about(key_of[1], (D, NRHS), 4.0, 24.0, ((0, 16), (1, 32)), jnp.float32)
    return dict(acts=acts, grads=grads)


damping = 1.0

def step_size(feature_count, token_count):
    return 1.0 / (damping + (1.0 + math.sqrt(feature_count / token_count)) ** 2)

def reference(acts, grads):
    token_count = acts.shape[0]
    omega_step = step_size(acts.shape[1], token_count)
    widened = acts.astype(jnp.float32)
    factor = jnp.dot(widened.T, widened, precision=lax.Precision.HIGHEST) / token_count
    applied = jnp.dot(factor, grads, precision=lax.Precision.HIGHEST) + damping * grads
    second = jnp.dot(factor, applied, precision=lax.Precision.HIGHEST) + damping * applied
    solution = 3.0 * omega_step * grads - 3.0 * omega_step ** 2 * applied + omega_step ** 3 * second
    return (factor, applied, solution)
```

```python
import math

import jax
import jax.numpy as jnp
from jax import lax
from jax.experimental import pallas as pl
from jax.experimental.pallas import tpu as pltpu
from jax.sharding import Mesh
from jax.sharding import PartitionSpec as P

AXES = ("zl", "x", "core", "y", "zh")
ROW = ("zl", "x", "core")
COL = ("y", "zh")
DAMPING = 1.0
F32 = jnp.float32
BF16 = jnp.bfloat16


def step_size(feature_count, token_count):
    return 1.0 / (DAMPING + (1.0 + math.sqrt(feature_count / token_count)) ** 2)


def two_terms(v):
    hi = v.astype(BF16)
    lo = (v - hi.astype(F32)).astype(BF16)
    return jnp.concatenate([hi, lo], axis=0)


def folded(p):
    n = p.shape[0] // 2
    return p[:n] + p[n:]


def kernel(
    tokens, omega, acts, grads, f_out, ap_out, sol_out,
    AC, AK, LB, GH, AP, APH, YS, R1, S2, R2, R3, APS, APT,
    zl_s, zl_r, x_s, x_r, sib_s, sib_r, zs_s, zs_r, xs_s, p_r, ys_s, ys_r,
    rs_s, rs_r, zh_s, zh_r, ag_s, ag_r, ap_s, ap_r,
):
    zl, x, core, y, zh = [lax.axis_index(a) for a in AXES]
    sib = 1 - core

    def plus(v, d):
        return lax.rem(v + d, 4)

    def dev(zl_=zl, x_=x, core_=core, y_=y, zh_=zh):
        return (zl_, x_, core_, y_, zh_)

    def send(src, dst, ss, rs, to):
        pltpu.make_async_remote_copy(
            src_ref=src, dst_ref=dst, send_sem=ss, recv_sem=rs,
            device_id=to, device_id_type=pl.DeviceIdType.MESH,
        ).start()

    def wait(ref, sem):
        pltpu.make_async_copy(ref, ref, sem).wait()

    barrier = pltpu.get_barrier_semaphore()

    def hello(to):
        pl.semaphore_signal(barrier, inc=1, device_id=to, device_id_type=pl.DeviceIdType.MESH)

    on_line = zl == y
    diagonal = jnp.logical_and(x == zh, y == zl)
    for d in (1, 2, 3):
        hello(dev(zl_=plus(zl, d)))
        hello(dev(x_=plus(x, d)))
        hello(dev(y_=plus(y, d)))
        hello(dev(zh_=plus(zh, d)))
    hello(dev(core_=sib))
    for dz in range(4):
        for dl in range(4):
            for dc in range(2):
                to = dev(zl_=plus(zl, dl), core_=lax.rem(core + dc, 2), y_=zl, zh_=plus(zh, dz))
                if dz == dl == dc == 0:
                    pl.when(jnp.logical_not(on_line))(lambda to=to: hello(to))
                else:
                    hello(to)
    mirror = [dev(zl_=y, x_=zh, core_=lax.rem(core + dc, 2), y_=zl, zh_=x) for dc in range(2)]
    pl.when(jnp.logical_not(diagonal))(lambda: hello(mirror[0]))
    hello(mirror[1])

    g = jnp.transpose(grads[...])
    GH[...] = two_terms(g)
    AP[...] = g

    greeted = 13 + 31 + 1
    pl.semaphore_wait(barrier, greeted + jnp.where(on_line, 0, 1) + jnp.where(diagonal, 0, 1))

    def spot(dx, dl):
        return AC.at[:, plus(x, 4 - dx), plus(zl, 4 - dl) * 2 + core]

    def sib_spot(dx, dl):
        return AC.at[:, plus(x, 4 - dx), plus(zl, 4 - dl) * 2 + sib]

    def to_x(src, dl):
        for d in (1, 3, 2):
            send(src, spot(0, dl), x_s, x_r.at[d - 1, dl], dev(x_=plus(x, d)))

    def to_sib(src, dx, dl):
        send(src, spot(dx, dl), sib_s, sib_r.at[dx, dl], dev(core_=sib))

    own = pltpu.make_async_copy(acts, spot(0, 0), ap_s.at[2])
    own.start()
    for d in (1, 3, 2):
        send(acts, spot(0, 0), zl_s, zl_r.at[d - 1], dev(zl_=plus(zl, d)))
    to_sib(acts, 0, 0)
    to_x(acts, 0)
    for dz in (0, 1, 3, 2):
        for dy in range(4):
            for dc in range(2):
                part = plus(y, dy)
                half = lax.rem(core + dc, 2)
                src = acts.at[part, :, pl.ds(pl.multiple_of(half * 512, 512), 512)]
                dst = LB.at[zh, zl * 2 + core]
                to = dev(zl_=y, core_=half, y_=part, zh_=plus(zh, dz))
                if dz == dy == dc == 0:
                    @pl.when(on_line)
                    def _():
                        pltpu.make_async_copy(src, dst, zs_r.at[0]).start()

                    @pl.when(jnp.logical_not(on_line))
                    def _():
                        send(src, dst, zs_s.at[1], zs_r.at[0], to)
                else:
                    send(src, dst, zs_s.at[0 if dz == 0 else 2], zs_r.at[dz], to)

    def pass_on(dz):
        wait(LB.at[0], zs_r.at[dz])
        block = plus(zh, 4 - dz)

        @pl.when(block == x)
        def _():
            pltpu.make_async_copy(LB.at[block], AK.at[y, x], p_r.at[x]).start()

        @pl.when(block != x)
        def _():
            send(LB.at[block], AK.at[y, x], xs_s, p_r.at[x], dev(x_=block))

    def tokens_of(dq):
        return AC[:, plus(x, 4 - dq)].reshape(512, 1024)

    def partial(ph, q, rhs):
        a = tokens_of(q)
        p = folded(lax.dot_general(rhs[...], a, (((1,), (1,)), ((), ())), preferred_element_type=F32))
        for j in range(4):
            YS[ph, q, j] = p[:, 128 * j : 128 * (j + 1)]
        for d in (1, 3, 2):
            to = plus(y, d)
            send(YS.at[ph, q, to], R1.at[ph, q, d - 1], rs_s.at[ph], rs_r.at[ph, q, d - 1], dev(y_=to))

    def cross(ph, q):
        s = YS[ph, q, y]
        for d in (1, 3, 2):
            wait(R1.at[ph, q, d - 1], rs_r.at[ph, q, d - 1])
            s = s + R1[ph, q, d - 1]
        S2[ph, q] = s
        for d in (1, 3, 2):
            send(S2.at[ph, q], R2.at[ph, q, d - 1], zh_s.at[ph], zh_r.at[ph, q, d - 1], dev(zh_=plus(zh, d)))

    def spread(ph, q):
        s = S2[ph, q]
        for d in (1, 3, 2):
            wait(R2.at[ph, q, d - 1], zh_r.at[ph, q, d - 1])
            s = s + R2[ph, q, d - 1]
        R3[ph, q, y] = s
        for d in (1, 3, 2):
            send(R3.at[ph, q, y], R3.at[ph, q, y], ag_s.at[ph], ag_r.at[ph, q, d - 1], dev(y_=plus(y, d)))

    def collect(ph, q):
        for d in (1, 3, 2):
            wait(R3.at[ph, q, 0], ag_r.at[ph, q, d - 1])
        v = jnp.concatenate([R3[ph, q, j] for j in range(4)], axis=1)
        return folded(jnp.dot(two_terms(v), tokens_of(q), preferred_element_type=F32))

    def sib_quarter(dx):
        for dl in range(4):
            wait(sib_spot(dx, dl), sib_r.at[dx, dl])

    for d in (1, 3, 2):
        wait(spot(0, d), zl_r.at[d - 1])
        to_x(spot(0, d), d)
        to_sib(spot(0, d), 0, d)
    own.wait()
    pass_on(0)
    sib_quarter(0)
    partial(0, 0, GH)
    for dx in (1, 3):
        for dl in (0, 1, 3, 2):
            wait(spot(dx, dl), x_r.at[dx - 1, dl])
            to_sib(spot(dx, dl), dx, dl)
    pass_on(1)
    pass_on(3)
    cross(0, 0)
    sib_quarter(1)
    partial(0, 1, GH)
    sib_quarter(3)
    partial(0, 3, GH)
    for dl in (0, 1, 3, 2):
        wait(spot(2, dl), x_r.at[1, dl])
        to_sib(spot(2, dl), 2, dl)
    cross(0, 1)
    sib_quarter(2)
    partial(0, 2, GH)
    cross(0, 3)
    pass_on(2)
    cross(0, 2)
    spread(0, 0)
    for k in range(4):
        wait(AK.at[y, k], p_r.at[k])
        for d in (1, 3, 2):
            send(AK.at[y, k], AK.at[y, k], ys_s, ys_r.at[d - 1], dev(y_=plus(y, d)))
    for q in (1, 3, 2):
        spread(0, q)
    total = collect(0, 0)
    for q in (1, 3, 2):
        total = total + collect(0, q)
    applied = total * (1.0 / tokens) + DAMPING * g
    APH[...] = two_terms(applied)
    for h in range(2):
        APS[h] = applied[:, 512 * h : 512 * (h + 1)]
    for q in (0, 1, 3, 2):
        partial(1, q, APH)
    for dc in range(2):
        half = lax.rem(core + dc, 2)
        if dc == 0:
            @pl.when(diagonal)
            def _():
                pltpu.make_async_copy(APS.at[half], APT.at[core], ap_r.at[0]).start()

            @pl.when(jnp.logical_not(diagonal))
            def _():
                send(APS.at[half], APT.at[core], ap_s.at[0], ap_r.at[0], mirror[0])
        else:
            send(APS.at[half], APT.at[core], ap_s.at[1], ap_r.at[1], mirror[1])
    for q in (0, 1, 3, 2):
        cross(1, q)
    for d in (1, 3, 2):
        wait(AK.at[0], ys_r.at[d - 1])
    scale = 1.0 / tokens

    def tile(t, _):
        at = pl.ds(pl.multiple_of(t * 128, 128), 128)
        left = AK[:, :, :, :, at].reshape(2048, 128)
        right = AC[...].reshape(2048, 1024)
        f_out[at, :] = (
            lax.dot_general(left, right, (((0,), (0,)), ((), ())), preferred_element_type=F32) * scale
        )
        return 0

    lax.fori_loop(0, 4, tile, 0)
    for q in (0, 1, 3, 2):
        spread(1, q)
    total = collect(1, 0)
    for q in (1, 3, 2):
        total = total + collect(1, q)
    sol_out[...] = (
        3.0 * omega * g
        + (omega**3 * DAMPING - 3.0 * omega**2) * applied
        + (omega**3 / tokens) * total
    )
    wait(APT.at[0], ap_r.at[0])
    wait(APT.at[0], ap_r.at[1])
    ap_out[...] = APT[...].reshape(32, 512)

    wait(AC.at[:, 0, 0:3], zl_s)
    wait(AC.at[:, 0:3, 0:4], x_s)
    wait(AC.at[:, 0:2], sib_s)
    wait(LB.at[0, 0:7], zs_s.at[0])
    pl.when(jnp.logical_not(on_line))(lambda: wait(LB.at[0, 0], zs_s.at[1]))
    wait(LB.at[0:3], zs_s.at[2])
    wait(LB.at[0:3], xs_s)
    wait(AK.at[0:3], ys_s)
    for ph in range(2):
        wait(R1.at[ph], rs_s.at[ph])
        wait(R1.at[ph], zh_s.at[ph])
        wait(R1.at[ph], ag_s.at[ph])
    pl.when(jnp.logical_not(diagonal))(lambda: wait(APT.at[0], ap_s.at[0]))
    wait(APT.at[0], ap_s.at[1])


def local(acts, grads):
    tokens = 2048
    omega = step_size(16384, tokens)
    dma = pltpu.SemaphoreType.DMA
    vmem = pl.BlockSpec(memory_space=pltpu.VMEM)

    def body(*refs):
        kernel(tokens, omega, *refs)

    factor, ap, sol = pl.pallas_call(
        body,
        out_shape=(
            jax.ShapeDtypeStruct((512, 1024), F32),
            jax.ShapeDtypeStruct((32, 512), F32),
            jax.ShapeDtypeStruct((16, 1024), F32),
        ),
        in_specs=[vmem, vmem],
        out_specs=[vmem, vmem, vmem],
        scratch_shapes=[
            pltpu.VMEM((4, 4, 8, 16, 1024), BF16),
            pltpu.VMEM((4, 4, 8, 16, 512), BF16),
            pltpu.VMEM((4, 8, 16, 512), BF16),
            pltpu.VMEM((32, 1024), BF16),
            pltpu.VMEM((16, 1024), F32),
            pltpu.VMEM((32, 1024), BF16),
            pltpu.VMEM((2, 4, 4, 16, 128), F32),
            pltpu.VMEM((2, 4, 3, 16, 128), F32),
            pltpu.VMEM((2, 4, 16, 128), F32),
            pltpu.VMEM((2, 4, 3, 16, 128), F32),
            pltpu.VMEM((2, 4, 4, 16, 128), F32),
            pltpu.VMEM((2, 16, 512), F32),
            pltpu.VMEM((2, 16, 512), F32),
            dma(()), dma((3,)), dma(()), dma((3, 4)), dma(()), dma((4, 4)),
            dma((3,)), dma((4,)), dma(()), dma((4,)), dma(()), dma((3,)),
            dma((2,)), dma((2, 4, 3)), dma((2,)), dma((2, 4, 3)), dma((2,)), dma((2, 4, 3)),
            dma((3,)), dma((2,)),
        ],
        compiler_params=pltpu.CompilerParams(
            collective_id=0, has_side_effects=True, vmem_limit_bytes=48 * 2**20
        ),
        name="everything",
    )(acts.reshape(4, 16, 1024), grads)
    return factor, ap.T, sol.T


def solution(mesh):
    split = Mesh(mesh.devices.reshape(4, 4, 2, 4, 4), AXES)
    return jax.shard_map(
        local,
        mesh=split,
        in_specs=(P(ROW, COL), P(COL, ROW)),
        out_specs=(P(ROW, COL), P(ROW, COL), P(COL, ROW)),
        check_vma=False,
    )
```

```python
import math

import jax
import jax.numpy as jnp
from jax import lax
from jax.experimental import pallas as pl
from jax.experimental.pallas import tpu as pltpu
from jax.sharding import Mesh
from jax.sharding import PartitionSpec as P

AXES = ("zl", "x", "core", "y", "zh")
ROW = ("zl", "x", "core")
COL = ("y", "zh")
DAMPING = 1.0
F32 = jnp.float32
BF16 = jnp.bfloat16


def step_size(feature_count, token_count):
    return 1.0 / (DAMPING + (1.0 + math.sqrt(feature_count / token_count)) ** 2)


def two_terms(v):
    hi = v.astype(BF16)
    lo = (v - hi.astype(F32)).astype(BF16)
    return jnp.concatenate([hi, lo], axis=0)


def folded(p):
    n = p.shape[0] // 2
    return p[:n] + p[n:]


def kernel(
    tokens, omega, acts, grads, f_out, ap_out, sol_out,
    AC, AK, LB, SC, GX, APH, YA, YP, P1, P2, P3, P4, YS, R1, S2, R2, R3, APS, APT,
    sc_s, sc_r, zl_s, zl_r, x_s, x_r, sib_s, sib_r, zs_s, zs_r, xs_s, p_r, ys_s, ys_r,
    gx_s, gx_r, p1_s, p1_r, p2_s, p2_r, ya_s, ya_r, rs_s, rs_r, zh_s, zh_r, ag_s, ag_r, ap_s, ap_r,
):
    zl, x, core, y, zh = [lax.axis_index(a) for a in AXES]
    sib = 1 - core

    def plus(v, d):
        return lax.rem(v + d, 4)

    def dev(zl_=zl, x_=x, core_=core, y_=y, zh_=zh):
        return (zl_, x_, core_, y_, zh_)

    def send(src, dst, ss, rs, to):
        pltpu.make_async_remote_copy(
            src_ref=src, dst_ref=dst, send_sem=ss, recv_sem=rs,
            device_id=to, device_id_type=pl.DeviceIdType.MESH,
        ).start()

    def wait(ref, sem):
        pltpu.make_async_copy(ref, ref, sem).wait()

    barrier = pltpu.get_barrier_semaphore()

    def hello(to):
        pl.semaphore_signal(barrier, inc=1, device_id=to, device_id_type=pl.DeviceIdType.MESH)

    diagonal = jnp.logical_and(x == zh, y == zl)
    for d in (1, 2, 3):
        hello(dev(zl_=plus(zl, d)))
        hello(dev(x_=plus(x, d)))
        hello(dev(y_=plus(y, d)))
        hello(dev(zh_=plus(zh, d)))
        for e in (1, 2, 3):
            hello(dev(x_=plus(x, d), y_=plus(y, e)))
        hello(dev(core_=sib, y_=plus(y, d)))
    hello(dev(core_=sib))
    for dz in range(4):
        for dl in range(4):
            if dz and dl:
                hello(dev(zl_=plus(zl, dl), zh_=plus(zh, dz)))
    mirror = [dev(zl_=y, x_=zh, core_=lax.rem(core + dc, 2), y_=zl, zh_=x) for dc in range(2)]
    pl.when(jnp.logical_not(diagonal))(lambda: hello(mirror[0]))
    hello(mirror[1])

    g = jnp.transpose(grads[...])
    GX[x] = two_terms(g)

    greeted = 13 + 9 + 3 + 9 + 1
    pl.semaphore_wait(barrier, greeted + jnp.where(diagonal, 0, 1))

    def spot(dx, dl):
        return AC.at[plus(x, 4 - dx), plus(zl, 4 - dl), :, core]

    def sib_spot(dx, dl):
        return AC.at[plus(x, 4 - dx), plus(zl, 4 - dl), :, sib]

    def to_x(src, dl):
        for d in (1, 3):
            send(src, spot(0, dl), x_s, x_r.at[d - 1, dl], dev(x_=plus(x, d)))

    def to_sib(src, dx, dl):
        send(src, spot(dx, dl), sib_s, sib_r.at[dx, dl], dev(core_=sib))

    def scatter():
        for dy in (1, 3, 2, 0):
            for dc in range(2):
                part, half = plus(y, dy), lax.rem(core + dc, 2)
                src = acts.at[part, :, pl.ds(pl.multiple_of(half * 512, 512), 512)]
                dst = SC.at[y, core]
                if dy or dc:
                    send(src, dst, sc_s, sc_r, dev(core_=half, y_=part))
                else:
                    pltpu.make_async_copy(src, dst, sc_r).start()

    def over_z(dz):
        dst = LB.at[zh, pl.ds(zl * 2, 2)]
        for dl in (1, 3, 2, 0):
            at = plus(zl, dl)
            if dz or dl:
                send(SC.at[at], dst, zs_s.at[0 if dz == 0 else 1], zs_r.at[dz], dev(zl_=at, zh_=plus(zh, dz)))
            else:
                pltpu.make_async_copy(SC.at[at], dst, zs_r.at[0]).start()

    def pass_on(dz):
        wait(LB.at[0], zs_r.at[dz])
        block = plus(zh, 4 - dz)

        @pl.when(block == x)
        def _():
            pltpu.make_async_copy(LB.at[block], AK.at[y, x], p_r.at[x]).start()

        @pl.when(block != x)
        def _():
            send(LB.at[block], AK.at[y, x], xs_s, p_r.at[x], dev(x_=block))

    def over_y(dz):
        @pl.when(plus(zh, 4 - dz) == x)
        def _():
            for k in range(4):
                wait(AK.at[y, k], p_r.at[k])
                for d in (1, 3):
                    send(AK.at[y, k], AK.at[y, k], ys_s, ys_r.at[d - 1, k], dev(y_=plus(y, d)))

    def wait_y(n, k):
        wait(AK.at[0, 0], ys_r.at[n - 1, k])

    def relay_y():
        for k in range(4):
            d = 1 if k < 2 else 3
            at = AK.at[plus(y, 4 - d), k]
            wait_y(d, k)
            send(at, at, ys_s, ys_r.at[1, k], dev(y_=plus(y, d)))

    def first_partial(dl):
        j = plus(zl, 4 - dl)
        a = AC[x, j].reshape(128, 1024)
        p = lax.dot_general(
            GX[...].reshape(128, 1024), a, (((1,), (1,)), ((), ())), preferred_element_type=F32
        ).reshape(4, 2, 16, 128)
        YP[j] = p[:, 0] + p[:, 1]

        @pl.when(j != y)
        def _():
            send(YP.at[j], P1.at[y], p1_s, p1_r.at[y], dev(y_=j))

    def first_cross():
        v = YP[y]
        for d in (1, 3, 2):
            at = plus(y, d)
            wait(P1.at[at], p1_r.at[at])
            v = v + P1[at]
        P2[...] = v
        for d in (2, 1, 3):
            send(P2, P3.at[d - 1], p2_s, p2_r.at[d - 1], dev(zh_=plus(zh, d)))

    def first_spread():
        v = P2[...]
        for d in (1, 3, 2):
            wait(P3.at[d - 1], p2_r.at[d - 1])
            v = v + P3[d - 1]
        P4[...] = v
        YA[x, y] = P4[x]
        for dx in (0, 1, 3, 2):
            for dy in (0, 1, 3, 2):
                if dx or dy:
                    xt = plus(x, dx)
                    send(P4.at[xt], YA.at[x, y], ya_s.at[1 if dx == 0 else 0], ya_r.at[dx, dy], dev(x_=xt, y_=plus(y, dy)))

    def product(pieces, q):
        v = jnp.concatenate(pieces, axis=1)
        a = AC[plus(x, 4 - q)].reshape(512, 1024)
        return folded(jnp.dot(two_terms(v), a, preferred_element_type=F32))

    def first_collect(q):
        for d in (0, 1, 3, 2):
            if q or d:
                wait(YA.at[0, 0], ya_r.at[q, d])
        xq = plus(x, 4 - q)
        return product([YA[xq, j] for j in range(4)], q)

    def partial(q):
        a = AC[plus(x, 4 - q)].reshape(512, 1024)
        p = folded(lax.dot_general(APH[...], a, (((1,), (1,)), ((), ())), preferred_element_type=F32))
        for j in range(4):
            YS[q, j] = p[:, 128 * j : 128 * (j + 1)]
        for d in (1, 3, 2):
            to = plus(y, d)
            send(YS.at[q, to], R1.at[q, d - 1], rs_s, rs_r.at[q, d - 1], dev(y_=to))

    def cross(q):
        v = YS[q, y]
        for d in (1, 3, 2):
            wait(R1.at[q, d - 1], rs_r.at[q, d - 1])
            v = v + R1[q, d - 1]
        S2[q] = v
        for d in (2, 1, 3):
            send(S2.at[q], R2.at[q, d - 1], zh_s, zh_r.at[q, d - 1], dev(zh_=plus(zh, d)))

    def spread(q):
        v = S2[q]
        for d in (1, 3, 2):
            wait(R2.at[q, d - 1], zh_r.at[q, d - 1])
            v = v + R2[q, d - 1]
        R3[q, y] = v
        for d in (1, 3, 2):
            send(R3.at[q, y], R3.at[q, y], ag_s, ag_r.at[q, d - 1], dev(y_=plus(y, d)))

    def collect(q):
        for d in (1, 3, 2):
            wait(R3.at[q, 0], ag_r.at[q, d - 1])
        return product([R3[q, j] for j in range(4)], q)

    def sib_quarter(dx):
        for dl in range(4):
            wait(sib_spot(dx, dl), sib_r.at[dx, dl])

    scale = 1.0 / tokens

    def factor_part(n):
        i = plus(y, 4 - n)

        def tile(t, _):
            at = pl.ds(pl.multiple_of(t * 128, 128), 128)
            left = AK[i, :, :, :, at].reshape(512, 128)
            right = AC[:, :, i].reshape(512, 1024)
            p = lax.dot_general(left, right, (((0,), (0,)), ((), ())), preferred_element_type=F32) * scale
            f_out[at, :] = p if n == 0 else f_out[at, :] + p
            return 0

        lax.fori_loop(0, 4, tile, 0)

    scatter()
    own = pltpu.make_async_copy(acts, spot(0, 0), ap_s.at[2])
    own.start()
    for d in (1, 3, 2):
        send(acts, spot(0, 0), zl_s, zl_r.at[d - 1], dev(zl_=plus(zl, d)))
    to_sib(acts, 0, 0)
    for d in (1, 3, 2):
        send(GX.at[x], GX.at[x], gx_s, gx_r.at[d - 1], dev(x_=plus(x, d)))
    to_x(acts, 0)
    for d in (1, 3, 2):
        wait(spot(0, d), zl_r.at[d - 1])
        to_x(spot(0, d), d)
        to_sib(spot(0, d), 0, d)
        if d == 1:
            own.wait()
            for e in (1, 3, 2):
                wait(GX.at[0], gx_r.at[e - 1])
            wait(sib_spot(0, 0), sib_r.at[0, 0])
            first_partial(0)
    for d in (1, 3, 2):
        wait(sib_spot(0, d), sib_r.at[0, d])
        first_partial(d)
    first_cross()
    wait(SC, sc_r)
    over_z(2)
    over_z(1)
    over_z(3)
    over_z(0)
    for dl in (0, 1, 3, 2):
        for dx in (1, 3):
            wait(spot(dx, dl), x_r.at[dx - 1, dl])
            if (dx == 1) == (dl < 2):
                send(spot(dx, dl), spot(dx, dl), x_s, x_r.at[1, dl], dev(x_=plus(x, dx)))
            to_sib(spot(dx, dl), dx, dl)
    first_spread()
    for dl in (0, 1, 3, 2):
        wait(spot(2, dl), x_r.at[1, dl])
        to_sib(spot(2, dl), 2, dl)
    pass_on(2)
    total = first_collect(0)
    for q in (1, 3, 2):
        sib_quarter(q)
        total = total + first_collect(q)
    applied = total * scale + DAMPING * g
    APH[...] = two_terms(applied)
    for h in range(2):
        APS[h] = applied[:, 512 * h : 512 * (h + 1)]
    for q in (0, 1, 3, 2):
        partial(q)
    pass_on(1)
    pass_on(3)
    pass_on(0)
    for q in (0, 1, 3, 2):
        cross(q)
    for dc in range(2):
        half = lax.rem(core + dc, 2)
        if dc == 0:
            @pl.when(diagonal)
            def _():
                pltpu.make_async_copy(APS.at[half], APT.at[core], ap_r.at[0]).start()

            @pl.when(jnp.logical_not(diagonal))
            def _():
                send(APS.at[half], APT.at[core], ap_s.at[0], ap_r.at[0], mirror[0])
        else:
            send(APS.at[half], APT.at[core], ap_s.at[1], ap_r.at[1], mirror[1])
    over_y(2)
    over_y(1)
    over_y(3)
    over_y(0)
    for q in (0, 1, 3, 2):
        spread(q)
    relay_y()
    factor_part(0)
    total = collect(0)
    for q in (1, 3, 2):
        total = total + collect(q)
    sol_out[...] = (
        3.0 * omega * g
        + (omega**3 * DAMPING - 3.0 * omega**2) * applied
        + (omega**3 / tokens) * total
    )
    wait(APT.at[0], ap_r.at[0])
    wait(APT.at[0], ap_r.at[1])
    ap_out[...] = APT[...].reshape(32, 512)
    for n in (1, 3, 2):
        for k in range(4):
            if n != 2 and (n == 1) == (k < 2):
                continue
            wait_y(n, k)
        factor_part(n)

    wait(AC.at[0:3, 0, :, 0], zl_s)
    wait(AC.at[0:3, :, :, 0], x_s)
    wait(AC.at[:, :, :, 0], sib_s)
    wait(LB.at[0, 0:7], sc_s)
    wait(LB.at[0, 0:6], zs_s.at[0])
    wait(LB.at[0:3], zs_s.at[1])
    wait(LB.at[0:3], xs_s)
    wait(AK.at[0:3], ys_s)
    wait(GX.at[0:3], gx_s)
    wait(P1.at[0:3], p1_s)
    wait(P3, p2_s)
    wait(YA.at[0:3], ya_s.at[0])
    wait(YA.at[0, 0:3], ya_s.at[1])
    wait(R1, rs_s)
    wait(R1, zh_s)
    wait(R1, ag_s)
    pl.when(jnp.logical_not(diagonal))(lambda: wait(APT.at[0], ap_s.at[0]))
    wait(APT.at[0], ap_s.at[1])


def local(acts, grads):
    tokens = 2048
    omega = step_size(16384, tokens)
    dma = pltpu.SemaphoreType.DMA
    vmem = pl.BlockSpec(memory_space=pltpu.VMEM)

    def body(*refs):
        kernel(tokens, omega, *refs)

    factor, ap, sol = pl.pallas_call(
        body,
        out_shape=(
            jax.ShapeDtypeStruct((512, 1024), F32),
            jax.ShapeDtypeStruct((32, 512), F32),
            jax.ShapeDtypeStruct((16, 1024), F32),
        ),
        in_specs=[vmem, vmem],
        out_specs=[vmem, vmem, vmem],
        scratch_shapes=[
            pltpu.VMEM((4, 4, 4, 2, 16, 1024), BF16),
            pltpu.VMEM((4, 4, 8, 16, 512), BF16),
            pltpu.VMEM((4, 8, 16, 512), BF16),
            pltpu.VMEM((4, 2, 16, 512), BF16),
            pltpu.VMEM((4, 32, 1024), BF16),
            pltpu.VMEM((32, 1024), BF16),
            pltpu.VMEM((4, 4, 16, 128), F32),
            pltpu.VMEM((4, 4, 16, 128), F32),
            pltpu.VMEM((4, 4, 16, 128), F32),
            pltpu.VMEM((4, 16, 128), F32),
            pltpu.VMEM((3, 4, 16, 128), F32),
            pltpu.VMEM((4, 16, 128), F32),
            pltpu.VMEM((4, 4, 16, 128), F32),
            pltpu.VMEM((4, 3, 16, 128), F32),
            pltpu.VMEM((4, 16, 128), F32),
            pltpu.VMEM((4, 3, 16, 128), F32),
            pltpu.VMEM((4, 4, 16, 128), F32),
            pltpu.VMEM((2, 16, 512), F32),
            pltpu.VMEM((2, 16, 512), F32),
            dma(()), dma(()), dma(()), dma((3,)), dma(()), dma((3, 4)), dma(()), dma((4, 4)),
            dma((2,)), dma((4,)), dma(()), dma((4,)), dma(()), dma((3, 4)),
            dma(()), dma((3,)), dma(()), dma((4,)), dma(()), dma((3,)), dma((2,)), dma((4, 4)),
            dma(()), dma((4, 3)), dma(()), dma((4, 3)), dma(()), dma((4, 3)),
            dma((3,)), dma((2,)),
        ],
        compiler_params=pltpu.CompilerParams(
            collective_id=0, has_side_effects=True, vmem_limit_bytes=48 * 2**20
        ),
        name="everything",
    )(acts.reshape(4, 16, 1024), grads)
    return factor, ap.T, sol.T


def solution(mesh):
    split = Mesh(mesh.devices.reshape(4, 4, 2, 4, 4), AXES)
    return jax.shard_map(
        local,
        mesh=split,
        in_specs=(P(ROW, COL), P(COL, ROW)),
        out_specs=(P(ROW, COL), P(ROW, COL), P(COL, ROW)),
        check_vma=False,
    )
```

```python
import math

import jax
import jax.numpy as jnp
from jax import lax
from jax.experimental import pallas as pl
from jax.experimental.pallas import tpu as pltpu
from jax.sharding import Mesh
from jax.sharding import PartitionSpec as P

AXES = ("zl", "x", "core", "y", "zh")
ROW = ("zl", "x", "core")
COL = ("y", "zh")
DAMPING = 1.0
F32 = jnp.float32
BF16 = jnp.bfloat16


def step_size(feature_count, token_count):
    return 1.0 / (DAMPING + (1.0 + math.sqrt(feature_count / token_count)) ** 2)


def two_terms(v):
    hi = v.astype(BF16)
    lo = (v - hi.astype(F32)).astype(BF16)
    return jnp.concatenate([hi, lo], axis=0)


def folded(p):
    n = p.shape[0] // 2
    return p[:n] + p[n:]


def kernel(
    tokens, omega, acts, grads, f_out, ap_out, sol_out,
    AC, AK, LB, SC, GR, GX, APH, YA, YP, P1, P2, P3, P4, YS, R1, S2, R2, R3, APS, APT,
    v_s, sc_s, sc_r, zl_s, zl_r, x_s, x_r, sib_s, sib_r, zs_s, zs_r, xs_s, p_r, ys_s, ys_r,
    gx_s, gx_r, p1_s, p1_r, p2_s, p2_r, ya_s, ya_r, rs_s, rs_r, zh_s, zh_r, ag_s, ag_r, ap_s, ap_r,
):
    zl, x, core, y, zh = [lax.axis_index(a) for a in AXES]
    sib = 1 - core

    def plus(v, d):
        return lax.rem(v + d, 4)

    def dev(zl_=zl, x_=x, core_=core, y_=y, zh_=zh):
        return (zl_, x_, core_, y_, zh_)

    def send(src, dst, ss, rs, to):
        pltpu.make_async_remote_copy(
            src_ref=src, dst_ref=dst, send_sem=ss, recv_sem=rs,
            device_id=to, device_id_type=pl.DeviceIdType.MESH,
        ).start()

    def wait(ref, sem):
        pltpu.make_async_copy(ref, ref, sem).wait()

    own = pltpu.make_async_copy(acts, AC.at[x, zl, :, core], ap_s.at[2])
    own.start()
    bring = pltpu.make_async_copy(grads, GR, ap_s.at[3])
    bring.start()

    barrier = pltpu.get_barrier_semaphore()

    def hello(to):
        pl.semaphore_signal(barrier, inc=1, device_id=to, device_id_type=pl.DeviceIdType.MESH)

    diagonal = jnp.logical_and(x == zh, y == zl)
    for d in (1, 2, 3):
        hello(dev(zl_=plus(zl, d)))
        hello(dev(x_=plus(x, d)))
        hello(dev(y_=plus(y, d)))
        hello(dev(zh_=plus(zh, d)))
        for e in (1, 2, 3):
            hello(dev(x_=plus(x, d), y_=plus(y, e)))
        hello(dev(core_=sib, y_=plus(y, d)))
    hello(dev(core_=sib))
    for dz in range(4):
        for dl in range(4):
            if dz and dl:
                hello(dev(zl_=plus(zl, dl), zh_=plus(zh, dz)))
    mirror = [dev(zl_=y, x_=zh, core_=lax.rem(core + dc, 2), y_=zl, zh_=x) for dc in range(2)]

    own.wait()
    bring.wait()
    g = GR[...]
    GX[x] = two_terms(g)

    pl.semaphore_wait(barrier, 13 + 9 + 3 + 9)

    def spot(dx, dl):
        return AC.at[plus(x, 4 - dx), plus(zl, 4 - dl), :, core]

    def sib_spot(dx, dl):
        return AC.at[plus(x, 4 - dx), plus(zl, 4 - dl), :, sib]

    def to_x(src, dl):
        for d in (1, 3):
            send(src, spot(0, dl), x_s, x_r.at[d - 1, dl], dev(x_=plus(x, d)))

    def to_sib(src, dx, dl):
        send(src, spot(dx, dl), sib_s, sib_r.at[dx, dl], dev(core_=sib))

    def scatter():
        for dy in (1, 3, 2, 0):
            for dc in range(2):
                part, half = plus(y, dy), lax.rem(core + dc, 2)
                src = AC.at[x, zl, part, core, :, pl.ds(pl.multiple_of(half * 512, 512), 512)]
                dst = SC.at[y, core]
                if dy or dc:
                    send(src, dst, sc_s, sc_r, dev(core_=half, y_=part))
                else:
                    pltpu.make_async_copy(src, dst, sc_r).start()

    def over_z(dz):
        dst = LB.at[zh, pl.ds(zl * 2, 2)]
        for dl in (1, 3, 2, 0):
            at = plus(zl, dl)
            if dz or dl:
                send(SC.at[at], dst, zs_s.at[0 if dz == 0 else 1], zs_r.at[dz], dev(zl_=at, zh_=plus(zh, dz)))
            else:
                pltpu.make_async_copy(SC.at[at], dst, zs_r.at[0]).start()

    def relay_z():
        for d, part in ((1, pl.ds(0, 4)), (3, pl.ds(4, 4))):
            at = LB.at[plus(zh, 4 - d), part]
            send(at, at, v_s, zs_r.at[2], dev(zh_=plus(zh, d)))

    def pass_on(dz):
        wait(LB.at[0], zs_r.at[dz])
        block = plus(zh, 4 - dz)

        @pl.when(block == x)
        def _():
            pltpu.make_async_copy(LB.at[block], AK.at[y, x], p_r.at[x]).start()

        @pl.when(block != x)
        def _():
            send(LB.at[block], AK.at[y, x], xs_s, p_r.at[x], dev(x_=block))

    def over_y(dz):
        @pl.when(plus(zh, 4 - dz) == x)
        def _():
            for k in range(4):
                wait(AK.at[y, k], p_r.at[k])
                for d in (1, 3):
                    send(AK.at[y, k], AK.at[y, k], ys_s, ys_r.at[d - 1, k], dev(y_=plus(y, d)))

    def wait_y(n, k):
        wait(AK.at[0, 0], ys_r.at[n - 1, k])

    def relay_y():
        for k in range(4):
            d = 1 if k < 2 else 3
            at = AK.at[plus(y, 4 - d), k]
            wait_y(d, k)
            send(at, at, ys_s, ys_r.at[1, k], dev(y_=plus(y, d)))

    def first_partial(dl):
        j = plus(zl, 4 - dl)
        a = AC[x, j].reshape(128, 1024)
        p = lax.dot_general(
            GX[...].reshape(128, 1024), a, (((1,), (1,)), ((), ())), preferred_element_type=F32
        ).reshape(4, 2, 16, 128)
        YP[j] = p[:, 0] + p[:, 1]

        @pl.when(j != y)
        def _():
            send(YP.at[j], P1.at[y], p1_s, p1_r.at[y], dev(y_=j))

    def first_cross():
        v = YP[y]
        for d in (1, 3, 2):
            at = plus(y, d)
            wait(P1.at[at], p1_r.at[at])
            v = v + P1[at]
        P2[...] = v
        for d in (2, 1, 3):
            send(P2, P3.at[d - 1], p2_s, p2_r.at[d - 1], dev(zh_=plus(zh, d)))

    def first_spread():
        v = P2[...]
        for d in (1, 3, 2):
            wait(P3.at[d - 1], p2_r.at[d - 1])
            v = v + P3[d - 1]
        P4[...] = v
        YA[x, y] = P4[x]
        for dx in (0, 1, 3, 2):
            for dy in (0, 1, 3, 2):
                if dx or dy:
                    xt = plus(x, dx)
                    send(P4.at[xt], YA.at[x, y], ya_s.at[1 if dx == 0 else 0], ya_r.at[dx, dy], dev(x_=xt, y_=plus(y, dy)))

    def product(pieces, q):
        v = jnp.concatenate(pieces, axis=1)
        a = AC[plus(x, 4 - q)].reshape(512, 1024)
        return folded(jnp.dot(two_terms(v), a, preferred_element_type=F32))

    def first_collect(q):
        for d in (0, 1, 3, 2):
            if q or d:
                wait(YA.at[0, 0], ya_r.at[q, d])
        xq = plus(x, 4 - q)
        return product([YA[xq, j] for j in range(4)], q)

    def partial(q):
        a = AC[plus(x, 4 - q)].reshape(512, 1024)
        p = folded(lax.dot_general(APH[...], a, (((1,), (1,)), ((), ())), preferred_element_type=F32))
        for j in range(4):
            YS[q, j] = p[:, 128 * j : 128 * (j + 1)]
        for d in (1, 3, 2):
            to = plus(y, d)
            send(YS.at[q, to], R1.at[q, d - 1], rs_s, rs_r.at[q, d - 1], dev(y_=to))

    def cross(q):
        v = YS[q, y]
        for d in (1, 3, 2):
            wait(R1.at[q, d - 1], rs_r.at[q, d - 1])
            v = v + R1[q, d - 1]
        S2[q] = v
        for d in (2, 1, 3):
            send(S2.at[q], R2.at[q, d - 1], zh_s, zh_r.at[q, d - 1], dev(zh_=plus(zh, d)))

    def spread(q):
        v = S2[q]
        for d in (1, 3, 2):
            wait(R2.at[q, d - 1], zh_r.at[q, d - 1])
            v = v + R2[q, d - 1]
        R3[q, y] = v
        for d in (1, 3, 2):
            send(R3.at[q, y], R3.at[q, y], ag_s, ag_r.at[q, d - 1], dev(y_=plus(y, d)))

    def collect(q):
        for d in (1, 3, 2):
            wait(R3.at[q, 0], ag_r.at[q, d - 1])
        return product([R3[q, j] for j in range(4)], q)

    def sib_quarter(dx):
        for dl in range(4):
            wait(sib_spot(dx, dl), sib_r.at[dx, dl])

    scale = 1.0 / tokens

    def factor_part(n):
        i = plus(y, 4 - n)

        def tile(t, _):
            at = pl.ds(pl.multiple_of(t * 128, 128), 128)
            left = AK[i, :, :, :, at].reshape(512, 128)
            right = AC[:, :, i].reshape(512, 1024)
            p = lax.dot_general(left, right, (((0,), (0,)), ((), ())), preferred_element_type=F32) * scale
            f_out[at, :] = p if n == 0 else f_out[at, :] + p
            return 0

        lax.fori_loop(0, 4, tile, 0)

    scatter()
    mine = spot(0, 0)
    for d in (1, 3, 2):
        send(mine, mine, zl_s, zl_r.at[d - 1], dev(zl_=plus(zl, d)))
    to_sib(mine, 0, 0)
    for d in (1, 3, 2):
        send(GX.at[x], GX.at[x], gx_s, gx_r.at[d - 1], dev(x_=plus(x, d)))
    to_x(mine, 0)
    for d in (1, 3, 2):
        wait(spot(0, d), zl_r.at[d - 1])
        to_x(spot(0, d), d)
        to_sib(spot(0, d), 0, d)
        if d == 1:
            for e in (1, 3, 2):
                wait(GX.at[0], gx_r.at[e - 1])
            wait(sib_spot(0, 0), sib_r.at[0, 0])
            first_partial(0)
    wait(SC, sc_r)
    over_z(1)
    over_z(3)
    for d in (1, 3, 2):
        wait(sib_spot(0, d), sib_r.at[0, d])
        first_partial(d)
    first_cross()
    over_z(0)
    for dl in (0, 1, 3, 2):
        for dx in (1, 3):
            wait(spot(dx, dl), x_r.at[dx - 1, dl])
            if (dx == 1) == (dl < 2):
                send(spot(dx, dl), spot(dx, dl), x_s, x_r.at[1, dl], dev(x_=plus(x, dx)))
            to_sib(spot(dx, dl), dx, dl)
    first_spread()
    pass_on(1)
    pass_on(3)
    relay_z()
    for dl in (0, 1, 3, 2):
        wait(spot(2, dl), x_r.at[1, dl])
        to_sib(spot(2, dl), 2, dl)
    total = first_collect(0)
    for q in (1, 3, 2):
        sib_quarter(q)
        total = total + first_collect(q)
    applied = total * scale + DAMPING * g
    APH[...] = two_terms(applied)
    for h in range(2):
        APS[h] = applied[:, 512 * h : 512 * (h + 1)]
    for q in (0, 1, 3, 2):
        partial(q)
    pass_on(0)
    pass_on(2)
    for q in (0, 1, 3, 2):
        cross(q)
    for dc in range(2):
        half = lax.rem(core + dc, 2)
        if dc == 0:
            @pl.when(diagonal)
            def _():
                pltpu.make_async_copy(APS.at[half], APT.at[core], ap_r.at[0]).start()

            @pl.when(jnp.logical_not(diagonal))
            def _():
                send(APS.at[half], APT.at[core], ap_s.at[0], ap_r.at[0], mirror[0])
        else:
            send(APS.at[half], APT.at[core], ap_s.at[1], ap_r.at[1], mirror[1])
    over_y(1)
    over_y(3)
    over_y(2)
    over_y(0)
    for q in (0, 1, 3, 2):
        spread(q)
    relay_y()
    factor_part(0)
    total = collect(0)
    for q in (1, 3, 2):
        total = total + collect(q)
    sol_out[...] = (
        3.0 * omega * g
        + (omega**3 * DAMPING - 3.0 * omega**2) * applied
        + (omega**3 / tokens) * total
    )
    wait(APT.at[0], ap_r.at[0])
    wait(APT.at[0], ap_r.at[1])
    ap_out[...] = APT[...].reshape(32, 512)
    for n in (1, 3, 2):
        for k in range(4):
            if n != 2 and (n == 1) == (k < 2):
                continue
            wait_y(n, k)
        factor_part(n)

    wait(AC.at[0:3, 0, :, 0], zl_s)
    wait(AC.at[0:3, :, :, 0], x_s)
    wait(AC.at[:, :, :, 0], sib_s)
    wait(LB.at[0, 0:7], sc_s)
    wait(LB.at[0, 0:6], zs_s.at[0])
    wait(LB.at[0:2], zs_s.at[1])
    wait(LB.at[0], v_s)
    wait(LB.at[0:3], xs_s)
    wait(AK.at[0:3], ys_s)
    wait(GX.at[0:3], gx_s)
    wait(P1.at[0:3], p1_s)
    wait(P3, p2_s)
    wait(YA.at[0:3], ya_s.at[0])
    wait(YA.at[0, 0:3], ya_s.at[1])
    wait(R1, rs_s)
    wait(R1, zh_s)
    wait(R1, ag_s)
    pl.when(jnp.logical_not(diagonal))(lambda: wait(APT.at[0], ap_s.at[0]))
    wait(APT.at[0], ap_s.at[1])


def local(acts, grads):
    tokens = 2048
    omega = step_size(16384, tokens)
    dma = pltpu.SemaphoreType.DMA
    vmem = pl.BlockSpec(memory_space=pltpu.VMEM)
    anywhere = pl.BlockSpec(memory_space=pltpu.HBM)

    def body(*refs):
        kernel(tokens, omega, *refs)

    factor, ap, sol = pl.pallas_call(
        body,
        out_shape=(
            jax.ShapeDtypeStruct((512, 1024), F32),
            jax.ShapeDtypeStruct((32, 512), F32),
            jax.ShapeDtypeStruct((16, 1024), F32),
        ),
        in_specs=[anywhere, anywhere],
        out_specs=[vmem, vmem, vmem],
        scratch_shapes=[
            pltpu.VMEM((4, 4, 4, 2, 16, 1024), BF16),
            pltpu.VMEM((4, 4, 8, 16, 512), BF16),
            pltpu.VMEM((4, 8, 16, 512), BF16),
            pltpu.VMEM((4, 2, 16, 512), BF16),
            pltpu.VMEM((16, 1024), F32),
            pltpu.VMEM((4, 32, 1024), BF16),
            pltpu.VMEM((32, 1024), BF16),
            pltpu.VMEM((4, 4, 16, 128), F32),
            pltpu.VMEM((4, 4, 16, 128), F32),
            pltpu.VMEM((4, 4, 16, 128), F32),
            pltpu.VMEM((4, 16, 128), F32),
            pltpu.VMEM((3, 4, 16, 128), F32),
            pltpu.VMEM((4, 16, 128), F32),
            pltpu.VMEM((4, 4, 16, 128), F32),
            pltpu.VMEM((4, 3, 16, 128), F32),
            pltpu.VMEM((4, 16, 128), F32),
            pltpu.VMEM((4, 3, 16, 128), F32),
            pltpu.VMEM((4, 4, 16, 128), F32),
            pltpu.VMEM((2, 16, 512), F32),
            pltpu.VMEM((2, 16, 512), F32),
            dma(()), dma(()), dma(()), dma(()), dma((3,)), dma(()), dma((3, 4)), dma(()), dma((4, 4)),
            dma((2,)), dma((4,)), dma(()), dma((4,)), dma(()), dma((3, 4)),
            dma(()), dma((3,)), dma(()), dma((4,)), dma(()), dma((3,)), dma((2,)), dma((4, 4)),
            dma(()), dma((4, 3)), dma(()), dma((4, 3)), dma(()), dma((4, 3)),
            dma((4,)), dma((2,)),
        ],
        compiler_params=pltpu.CompilerParams(
            collective_id=0, has_side_effects=True, vmem_limit_bytes=48 * 2**20
        ),
        name="everything",
    )(acts.reshape(4, 16, 1024), grads.T)
    return factor, ap.T, sol.T


def solution(mesh):
    split = Mesh(mesh.devices.reshape(4, 4, 2, 4, 4), AXES)
    return jax.shard_map(
        local,
        mesh=split,
        in_specs=(P(ROW, COL), P(COL, ROW)),
        out_specs=(P(ROW, COL), P(ROW, COL), P(COL, ROW)),
        check_vma=False,
    )
```

```python
import math

import jax
import jax.numpy as jnp
from jax import lax
from jax.experimental import pallas as pl
from jax.experimental.pallas import tpu as pltpu
from jax.sharding import Mesh
from jax.sharding import PartitionSpec as P

AXES = ("zl", "x", "core", "y", "zh")
ROW = ("zl", "x", "core")
COL = ("y", "zh")
DAMPING = 1.0
F32 = jnp.float32
BF16 = jnp.bfloat16


def step_size(feature_count, token_count):
    return 1.0 / (DAMPING + (1.0 + math.sqrt(feature_count / token_count)) ** 2)


def two_terms(v):
    hi = v.astype(BF16)
    lo = (v - hi.astype(F32)).astype(BF16)
    return jnp.concatenate([hi, lo], axis=0)


def folded(p):
    n = p.shape[0] // 2
    return p[:n] + p[n:]


def kernel(
    tokens, omega, acts, grads, f_out, ap_out, sol_out,
    AC, AK, LB, SC, GR, GX, APH, YA, YP, P1, P2, P3, P4, YS, R1, S2, R2, R3, APS, APT,
    v_s, sc_s, sc_r, zl_s, zl_r, x_s, x_r, sib_s, sib_r, zs_s, zs_r, xs_s, p_r, ys_s, ys_r,
    gx_s, gx_r, p1_s, p1_r, p2_s, p2_r, ya_s, ya_r, rs_s, rs_r, zh_s, zh_r, ag_s, ag_r, ap_s, ap_r,
):
    zl, x, core, y, zh = [lax.axis_index(a) for a in AXES]
    sib = 1 - core

    def plus(v, d):
        return lax.rem(v + d, 4)

    def dev(zl_=zl, x_=x, core_=core, y_=y, zh_=zh):
        return (zl_, x_, core_, y_, zh_)

    def send(src, dst, ss, rs, to):
        pltpu.make_async_remote_copy(
            src_ref=src, dst_ref=dst, send_sem=ss, recv_sem=rs,
            device_id=to, device_id_type=pl.DeviceIdType.MESH,
        ).start()

    def wait(ref, sem):
        pltpu.make_async_copy(ref, ref, sem).wait()

    own = pltpu.make_async_copy(acts, AC.at[x, zl, :, core], ap_s.at[2])
    own.start()
    bring = pltpu.make_async_copy(grads, GR, ap_s.at[3])
    bring.start()

    barrier = pltpu.get_barrier_semaphore()

    def hello(to):
        pl.semaphore_signal(barrier, inc=1, device_id=to, device_id_type=pl.DeviceIdType.MESH)

    diagonal = jnp.logical_and(x == zh, y == zl)
    for d in (1, 2, 3):
        hello(dev(zl_=plus(zl, d)))
        hello(dev(x_=plus(x, d)))
        hello(dev(y_=plus(y, d)))
        hello(dev(zh_=plus(zh, d)))
        for e in (1, 2, 3):
            hello(dev(x_=plus(x, d), y_=plus(y, e)))
        hello(dev(core_=sib, y_=plus(y, d)))
    hello(dev(core_=sib))
    for dz in range(4):
        for dl in range(4):
            if dz in (1, 3) and dl:
                hello(dev(zl_=plus(zl, dl), zh_=plus(zh, dz)))
    mirror = [dev(zl_=y, x_=zh, core_=lax.rem(core + dc, 2), y_=zl, zh_=x) for dc in range(2)]

    own.wait()
    bring.wait()
    g = GR[...]
    GX[x] = two_terms(g)

    pl.semaphore_wait(barrier, 13 + 9 + 3 + 6)

    def spot(dx, dl):
        return AC.at[plus(x, 4 - dx), plus(zl, 4 - dl), :, core]

    def sib_spot(dx, dl):
        return AC.at[plus(x, 4 - dx), plus(zl, 4 - dl), :, sib]

    def to_x(src, dl):
        for d in (1, 3):
            send(src, spot(0, dl), x_s, x_r.at[d - 1, dl], dev(x_=plus(x, d)))

    def to_sib(src, dx, dl):
        send(src, spot(dx, dl), sib_s, sib_r.at[dx, dl], dev(core_=sib))

    def scatter():
        for dy in (1, 3, 2, 0):
            for dc in range(2):
                part, half = plus(y, dy), lax.rem(core + dc, 2)
                src = AC.at[x, zl, part, core, :, pl.ds(pl.multiple_of(half * 512, 512), 512)]
                dst = SC.at[y, core]
                if dy or dc:
                    send(src, dst, sc_s, sc_r, dev(core_=half, y_=part))
                else:
                    pltpu.make_async_copy(src, dst, sc_r).start()

    def over_z(dz):
        dst = LB.at[zh, pl.ds(zl * 2, 2)]
        for dl in (1, 3, 2, 0):
            at = plus(zl, dl)
            if dz or dl:
                send(SC.at[at], dst, zs_s.at[0 if dz == 0 else 1], zs_r.at[dz], dev(zl_=at, zh_=plus(zh, dz)))
            else:
                pltpu.make_async_copy(SC.at[at], dst, zs_r.at[0]).start()

    def relay_z():
        for d, part in ((1, pl.ds(0, 4)), (3, pl.ds(4, 4))):
            at = LB.at[plus(zh, 4 - d), part]
            send(at, at, v_s, zs_r.at[2], dev(zh_=plus(zh, d)))

    def pass_on(dz):
        wait(LB.at[0], zs_r.at[dz])
        block = plus(zh, 4 - dz)

        @pl.when(block == x)
        def _():
            pltpu.make_async_copy(LB.at[block], AK.at[y, x], p_r.at[x]).start()

        @pl.when(block != x)
        def _():
            send(LB.at[block], AK.at[y, x], xs_s, p_r.at[x], dev(x_=block))

    def over_y(dz):
        @pl.when(plus(zh, 4 - dz) == x)
        def _():
            for k in range(4):
                wait(AK.at[y, k], p_r.at[k])
                for d in (1, 3):
                    send(AK.at[y, k], AK.at[y, k], ys_s, ys_r.at[d - 1, k], dev(y_=plus(y, d)))

    def wait_y(n, k):
        wait(AK.at[0, 0], ys_r.at[n - 1, k])

    def relay_y():
        for k in range(4):
            d = 1 if k < 2 else 3
            at = AK.at[plus(y, 4 - d), k]
            wait_y(d, k)
            send(at, at, ys_s, ys_r.at[1, k], dev(y_=plus(y, d)))

    def first_partial(dl):
        j = plus(zl, 4 - dl)
        a = AC[x, j].reshape(128, 1024)
        p = lax.dot_general(
            GX[...].reshape(128, 1024), a, (((1,), (1,)), ((), ())), preferred_element_type=F32
        ).reshape(4, 2, 16, 128)
        YP[j] = p[:, 0] + p[:, 1]

        @pl.when(j != y)
        def _():
            send(YP.at[j], P1.at[y], p1_s, p1_r.at[y], dev(y_=j))

    def first_cross():
        v = YP[y]
        for d in (1, 3, 2):
            at = plus(y, d)
            wait(P1.at[at], p1_r.at[at])
            v = v + P1[at]
        P2[...] = v
        for d in (2, 1, 3):
            send(P2, P3.at[d - 1], p2_s, p2_r.at[d - 1], dev(zh_=plus(zh, d)))

    def first_spread():
        v = P2[...]
        for d in (1, 3, 2):
            wait(P3.at[d - 1], p2_r.at[d - 1])
            v = v + P3[d - 1]
        P4[...] = v
        YA[x, y] = P4[x]
        for dx in (0, 1, 3, 2):
            for dy in (0, 1, 3, 2):
                if dx or dy:
                    xt = plus(x, dx)
                    send(P4.at[xt], YA.at[x, y], ya_s.at[1 if dx == 0 else 0], ya_r.at[dx, dy], dev(x_=xt, y_=plus(y, dy)))

    def product(pieces, q):
        v = jnp.concatenate(pieces, axis=1)
        a = AC[plus(x, 4 - q)].reshape(512, 1024)
        return folded(jnp.dot(two_terms(v), a, preferred_element_type=F32))

    def first_collect(q):
        for d in (0, 1, 3, 2):
            if q or d:
                wait(YA.at[0, 0], ya_r.at[q, d])
        xq = plus(x, 4 - q)
        return product([YA[xq, j] for j in range(4)], q)

    def partial(q):
        a = AC[plus(x, 4 - q)].reshape(512, 1024)
        p = folded(lax.dot_general(APH[...], a, (((1,), (1,)), ((), ())), preferred_element_type=F32))
        for j in range(4):
            YS[q, j] = p[:, 128 * j : 128 * (j + 1)]
        for d in (1, 3, 2):
            to = plus(y, d)
            send(YS.at[q, to], R1.at[q, d - 1], rs_s, rs_r.at[q, d - 1], dev(y_=to))

    def cross(q):
        v = YS[q, y]
        for d in (1, 3, 2):
            wait(R1.at[q, d - 1], rs_r.at[q, d - 1])
            v = v + R1[q, d - 1]
        S2[q] = v
        for d in (2, 1, 3):
            send(S2.at[q], R2.at[q, d - 1], zh_s, zh_r.at[q, d - 1], dev(zh_=plus(zh, d)))

    def spread(q):
        v = S2[q]
        for d in (1, 3, 2):
            wait(R2.at[q, d - 1], zh_r.at[q, d - 1])
            v = v + R2[q, d - 1]
        R3[q, y] = v
        for d in (1, 3, 2):
            send(R3.at[q, y], R3.at[q, y], ag_s, ag_r.at[q, d - 1], dev(y_=plus(y, d)))

    def collect(q):
        for d in (1, 3, 2):
            wait(R3.at[q, 0], ag_r.at[q, d - 1])
        return product([R3[q, j] for j in range(4)], q)

    def sib_quarter(dx):
        for dl in range(4):
            wait(sib_spot(dx, dl), sib_r.at[dx, dl])

    scale = 1.0 / tokens

    def factor_part(n):
        i = plus(y, 4 - n)

        def tile(t, _):
            at = pl.ds(pl.multiple_of(t * 128, 128), 128)
            left = AK[i, :, :, :, at].reshape(512, 128)
            right = AC[:, :, i].reshape(512, 1024)
            p = lax.dot_general(left, right, (((0,), (0,)), ((), ())), preferred_element_type=F32) * scale
            f_out[at, :] = p if n == 0 else f_out[at, :] + p
            return 0

        lax.fori_loop(0, 4, tile, 0)

    scatter()
    mine = spot(0, 0)
    for d in (1, 3, 2):
        send(mine, mine, zl_s, zl_r.at[d - 1], dev(zl_=plus(zl, d)))
    to_sib(mine, 0, 0)
    for d in (1, 3, 2):
        send(GX.at[x], GX.at[x], gx_s, gx_r.at[d - 1], dev(x_=plus(x, d)))
    to_x(mine, 0)
    for d in (1, 3, 2):
        wait(spot(0, d), zl_r.at[d - 1])
        to_x(spot(0, d), d)
        to_sib(spot(0, d), 0, d)
        if d == 1:
            for e in (1, 3, 2):
                wait(GX.at[0], gx_r.at[e - 1])
            wait(sib_spot(0, 0), sib_r.at[0, 0])
            first_partial(0)
    wait(SC, sc_r)
    over_z(1)
    over_z(3)
    for d in (1, 3, 2):
        wait(sib_spot(0, d), sib_r.at[0, d])
        first_partial(d)
    first_cross()
    over_z(0)
    for dl in (0, 1, 3, 2):
        for dx in (1, 3):
            wait(spot(dx, dl), x_r.at[dx - 1, dl])
            if (dx == 1) == (dl < 2):
                send(spot(dx, dl), spot(dx, dl), x_s, x_r.at[1, dl], dev(x_=plus(x, dx)))
            to_sib(spot(dx, dl), dx, dl)
    first_spread()
    pass_on(1)
    pass_on(3)
    relay_z()
    for dl in (0, 1, 3, 2):
        wait(spot(2, dl), x_r.at[1, dl])
        to_sib(spot(2, dl), 2, dl)
    total = first_collect(0)
    for q in (1, 3, 2):
        sib_quarter(q)
        total = total + first_collect(q)
    applied = total * scale + DAMPING * g
    APH[...] = two_terms(applied)
    for h in range(2):
        APS[h] = applied[:, 512 * h : 512 * (h + 1)]
    for q in (0, 1, 3, 2):
        partial(q)
    pass_on(0)
    pass_on(2)
    for q in (0, 1, 3, 2):
        cross(q)
    over_y(1)
    over_y(3)
    over_y(2)
    over_y(0)
    for dc in range(2):
        half = lax.rem(core + dc, 2)
        if dc == 0:
            @pl.when(diagonal)
            def _():
                pltpu.make_async_copy(APS.at[half], APT.at[core], ap_r.at[0]).start()

            @pl.when(jnp.logical_not(diagonal))
            def _():
                send(APS.at[half], APT.at[core], ap_s.at[0], ap_r.at[0], mirror[0])
        else:
            send(APS.at[half], APT.at[core], ap_s.at[1], ap_r.at[1], mirror[1])
    for q in (0, 1, 3, 2):
        spread(q)
    relay_y()
    factor_part(0)
    total = collect(0)
    for q in (1, 3, 2):
        total = total + collect(q)
    sol_out[...] = (
        3.0 * omega * g
        + (omega**3 * DAMPING - 3.0 * omega**2) * applied
        + (omega**3 / tokens) * total
    )
    wait(APT.at[0], ap_r.at[0])
    wait(APT.at[0], ap_r.at[1])
    ap_out[...] = APT[...].reshape(32, 512)
    for n in (1, 3, 2):
        for k in range(4):
            if n != 2 and (n == 1) == (k < 2):
                continue
            wait_y(n, k)
        factor_part(n)

    wait(AC.at[0:3, 0, :, 0], zl_s)
    wait(AC.at[0:3, :, :, 0], x_s)
    wait(AC.at[:, :, :, 0], sib_s)
    wait(LB.at[0, 0:7], sc_s)
    wait(LB.at[0, 0:6], zs_s.at[0])
    wait(LB.at[0:2], zs_s.at[1])
    wait(LB.at[0], v_s)
    wait(LB.at[0:3], xs_s)
    wait(AK.at[0:3], ys_s)
    wait(GX.at[0:3], gx_s)
    wait(P1.at[0:3], p1_s)
    wait(P3, p2_s)
    wait(YA.at[0:3], ya_s.at[0])
    wait(YA.at[0, 0:3], ya_s.at[1])
    wait(R1, rs_s)
    wait(R1, zh_s)
    wait(R1, ag_s)
    pl.when(jnp.logical_not(diagonal))(lambda: wait(APT.at[0], ap_s.at[0]))
    wait(APT.at[0], ap_s.at[1])


def local(acts, grads):
    tokens = 2048
    omega = step_size(16384, tokens)
    dma = pltpu.SemaphoreType.DMA
    vmem = pl.BlockSpec(memory_space=pltpu.VMEM)
    anywhere = pl.BlockSpec(memory_space=pltpu.HBM)

    def body(*refs):
        kernel(tokens, omega, *refs)

    factor, ap, sol = pl.pallas_call(
        body,
        out_shape=(
            jax.ShapeDtypeStruct((512, 1024), F32),
            jax.ShapeDtypeStruct((32, 512), F32),
            jax.ShapeDtypeStruct((16, 1024), F32),
        ),
        in_specs=[anywhere, anywhere],
        out_specs=[vmem, vmem, vmem],
        scratch_shapes=[
            pltpu.VMEM((4, 4, 4, 2, 16, 1024), BF16),
            pltpu.VMEM((4, 4, 8, 16, 512), BF16),
            pltpu.VMEM((4, 8, 16, 512), BF16),
            pltpu.VMEM((4, 2, 16, 512), BF16),
            pltpu.VMEM((16, 1024), F32),
            pltpu.VMEM((4, 32, 1024), BF16),
            pltpu.VMEM((32, 1024), BF16),
            pltpu.VMEM((4, 4, 16, 128), F32),
            pltpu.VMEM((4, 4, 16, 128), F32),
            pltpu.VMEM((4, 4, 16, 128), F32),
            pltpu.VMEM((4, 16, 128), F32),
            pltpu.VMEM((3, 4, 16, 128), F32),
            pltpu.VMEM((4, 16, 128), F32),
            pltpu.VMEM((4, 4, 16, 128), F32),
            pltpu.VMEM((4, 3, 16, 128), F32),
            pltpu.VMEM((4, 16, 128), F32),
            pltpu.VMEM((4, 3, 16, 128), F32),
            pltpu.VMEM((4, 4, 16, 128), F32),
            pltpu.VMEM((2, 16, 512), F32),
            pltpu.VMEM((2, 16, 512), F32),
            dma(()), dma(()), dma(()), dma(()), dma((3,)), dma(()), dma((3, 4)), dma(()), dma((4, 4)),
            dma((2,)), dma((4,)), dma(()), dma((4,)), dma(()), dma((3, 4)),
            dma(()), dma((3,)), dma(()), dma((4,)), dma(()), dma((3,)), dma((2,)), dma((4, 4)),
            dma(()), dma((4, 3)), dma(()), dma((4, 3)), dma(()), dma((4, 3)),
            dma((4,)), dma((2,)),
        ],
        compiler_params=pltpu.CompilerParams(
            collective_id=0, has_side_effects=True, vmem_limit_bytes=48 * 2**20
        ),
        name="everything",
    )(acts.reshape(4, 16, 1024), grads.T)
    return factor, ap.T, sol.T


def solution(mesh):
    split = Mesh(mesh.devices.reshape(4, 4, 2, 4, 4), AXES)
    return jax.shard_map(
        local,
        mesh=split,
        in_specs=(P(ROW, COL), P(COL, ROW)),
        out_specs=(P(ROW, COL), P(ROW, COL), P(COL, ROW)),
        check_vma=False,
    )
```

```python
import math

import jax
import jax.numpy as jnp
from jax import lax
from jax.experimental import pallas as pl
from jax.experimental.pallas import tpu as pltpu
from jax.sharding import Mesh
from jax.sharding import PartitionSpec as P

AXES = ("zl", "x", "core", "y", "zh")
ROW = ("zl", "x", "core")
COL = ("y", "zh")
DAMPING = 1.0
F32 = jnp.float32
BF16 = jnp.bfloat16


def step_size(feature_count, token_count):
    return 1.0 / (DAMPING + (1.0 + math.sqrt(feature_count / token_count)) ** 2)


def two_terms(v):
    hi = v.astype(BF16)
    lo = (v - hi.astype(F32)).astype(BF16)
    return jnp.concatenate([hi, lo], axis=0)


def folded(p):
    n = p.shape[0] // 2
    return p[:n] + p[n:]


def kernel(
    tokens, omega, acts, grads, f_out, ap_out, sol_out,
    AC, AK, LB, SC, GR, GX, APH, YA, YP, P1, P2, P3, P4, YS, R1, S2, R2, R3, APS, APT,
    v_s, sc_s, sc_r, zl_s, zl_r, x_s, x_r, sib_s, sib_r, zs_s, zs_r, xs_s, p_r, ys_s, ys_r,
    gx_s, gx_r, p1_s, p1_r, p2_s, p2_r, ya_s, ya_r, rs_s, rs_r, zh_s, zh_r, ag_s, ag_r, ap_s, ap_r,
):
    zl, x, core, y, zh = [lax.axis_index(a) for a in AXES]
    sib = 1 - core

    def plus(v, d):
        return lax.rem(v + d, 4)

    def dev(zl_=zl, x_=x, core_=core, y_=y, zh_=zh):
        return (zl_, x_, core_, y_, zh_)

    def send(src, dst, ss, rs, to):
        pltpu.make_async_remote_copy(
            src_ref=src, dst_ref=dst, send_sem=ss, recv_sem=rs,
            device_id=to, device_id_type=pl.DeviceIdType.MESH,
        ).start()

    def wait(ref, sem):
        pltpu.make_async_copy(ref, ref, sem).wait()

    own = pltpu.make_async_copy(acts, AC.at[x, zl, :, core], ap_s.at[2])
    own.start()
    bring = pltpu.make_async_copy(grads, GR, ap_s.at[3])
    bring.start()

    barrier = pltpu.get_barrier_semaphore()

    def hello(to):
        pl.semaphore_signal(barrier, inc=1, device_id=to, device_id_type=pl.DeviceIdType.MESH)

    diagonal = jnp.logical_and(x == zh, y == zl)
    for d in (1, 2, 3):
        hello(dev(zl_=plus(zl, d)))
        hello(dev(x_=plus(x, d)))
        hello(dev(y_=plus(y, d)))
        hello(dev(zh_=plus(zh, d)))
        for e in (1, 2, 3):
            hello(dev(x_=plus(x, d), y_=plus(y, e)))
        hello(dev(core_=sib, y_=plus(y, d)))
    hello(dev(core_=sib))
    for dz in range(4):
        for dl in range(4):
            if dz in (1, 3) and dl:
                hello(dev(zl_=plus(zl, dl), zh_=plus(zh, dz)))
    mirror = [dev(zl_=y, x_=zh, core_=lax.rem(core + dc, 2), y_=zl, zh_=x) for dc in range(2)]

    own.wait()
    bring.wait()
    g = GR[...]
    GX[x] = two_terms(g)

    pl.semaphore_wait(barrier, 13 + 9 + 3 + 6)

    def spot(dx, dl):
        return AC.at[plus(x, 4 - dx), plus(zl, 4 - dl), :, core]

    def sib_spot(dx, dl):
        return AC.at[plus(x, 4 - dx), plus(zl, 4 - dl), :, sib]

    def to_x(src, dl):
        for d in (1, 3):
            send(src, spot(0, dl), x_s, x_r.at[d - 1, dl], dev(x_=plus(x, d)))

    def to_sib(src, dx, dl):
        send(src, spot(dx, dl), sib_s, sib_r.at[dx, dl], dev(core_=sib))

    def scatter():
        for dy in (1, 3, 2, 0):
            for dc in range(2):
                part, half = plus(y, dy), lax.rem(core + dc, 2)
                src = AC.at[x, zl, part, core, :, pl.ds(pl.multiple_of(half * 512, 512), 512)]
                dst = SC.at[y, core]
                if dy or dc:
                    send(src, dst, sc_s, sc_r, dev(core_=half, y_=part))
                else:
                    pltpu.make_async_copy(src, dst, sc_r).start()

    def over_z(dz):
        dst = LB.at[zh, pl.ds(zl * 2, 2)]
        for dl in (1, 3, 2, 0):
            at = plus(zl, dl)
            if dz or dl:
                send(SC.at[at], dst, zs_s.at[0 if dz == 0 else 1], zs_r.at[dz], dev(zl_=at, zh_=plus(zh, dz)))
            else:
                pltpu.make_async_copy(SC.at[at], dst, zs_r.at[0]).start()

    def relay_z():
        for d, part in ((1, pl.ds(0, 4)), (3, pl.ds(4, 4))):
            at = LB.at[plus(zh, 4 - d), part]
            send(at, at, v_s, zs_r.at[2], dev(zh_=plus(zh, d)))

    def pass_on(dz):
        wait(LB.at[0], zs_r.at[dz])
        block = plus(zh, 4 - dz)

        @pl.when(block == x)
        def _():
            pltpu.make_async_copy(LB.at[block], AK.at[y, x], p_r.at[x]).start()

        @pl.when(block != x)
        def _():
            send(LB.at[block], AK.at[y, x], xs_s, p_r.at[x], dev(x_=block))

    def over_y(dz):
        @pl.when(plus(zh, 4 - dz) == x)
        def _():
            for k in range(4):
                wait(AK.at[y, k], p_r.at[k])
                for d in (1, 3):
                    send(AK.at[y, k], AK.at[y, k], ys_s, ys_r.at[d - 1, k], dev(y_=plus(y, d)))

    def wait_y(n, k):
        wait(AK.at[0, 0], ys_r.at[n - 1, k])

    def relay_y():
        for k in range(4):
            d = 1 if k < 2 else 3
            at = AK.at[plus(y, 4 - d), k]
            wait_y(d, k)
            send(at, at, ys_s, ys_r.at[1, k], dev(y_=plus(y, d)))

    def first_partial(dl):
        j = plus(zl, 4 - dl)
        a = AC[x, j].reshape(128, 1024)
        p = lax.dot_general(
            GX[...].reshape(128, 1024), a, (((1,), (1,)), ((), ())), preferred_element_type=F32
        ).reshape(4, 2, 16, 128)
        YP[j] = p[:, 0] + p[:, 1]

        @pl.when(j != y)
        def _():
            send(YP.at[j], P1.at[y], p1_s, p1_r.at[y], dev(y_=j))

    def first_cross():
        v = YP[y]
        for d in (1, 3, 2):
            at = plus(y, d)
            wait(P1.at[at], p1_r.at[at])
            v = v + P1[at]
        P2[...] = v
        for d in (2, 1, 3):
            send(P2, P3.at[d - 1], p2_s, p2_r.at[d - 1], dev(zh_=plus(zh, d)))

    def first_spread():
        v = P2[...]
        for d in (1, 3, 2):
            wait(P3.at[d - 1], p2_r.at[d - 1])
            v = v + P3[d - 1]
        P4[...] = v
        YA[x, y] = P4[x]
        for dx in (0, 1, 3, 2):
            for dy in (0, 1, 3, 2):
                if dx or dy:
                    xt = plus(x, dx)
                    send(P4.at[xt], YA.at[x, y], ya_s.at[1 if dx == 0 else 0], ya_r.at[dx, dy], dev(x_=xt, y_=plus(y, dy)))

    def product(pieces, q):
        v = jnp.concatenate(pieces, axis=1)
        a = AC[plus(x, 4 - q)].reshape(512, 1024)
        return folded(jnp.dot(two_terms(v), a, preferred_element_type=F32))

    def first_collect(q):
        for d in (0, 1, 3, 2):
            if q or d:
                wait(YA.at[0, 0], ya_r.at[q, d])
        xq = plus(x, 4 - q)
        return product([YA[xq, j] for j in range(4)], q)

    def partial(q):
        a = AC[plus(x, 4 - q)].reshape(512, 1024)
        p = folded(lax.dot_general(APH[...], a, (((1,), (1,)), ((), ())), preferred_element_type=F32))
        for j in range(4):
            YS[q, j] = p[:, 128 * j : 128 * (j + 1)]
        for d in (1, 3, 2):
            to = plus(y, d)
            send(YS.at[q, to], R1.at[q, d - 1], rs_s, rs_r.at[q, d - 1], dev(y_=to))

    def cross(q):
        v = YS[q, y]
        for d in (1, 3, 2):
            wait(R1.at[q, d - 1], rs_r.at[q, d - 1])
            v = v + R1[q, d - 1]
        S2[q] = v
        for d in (2, 1, 3):
            send(S2.at[q], R2.at[q, d - 1], zh_s, zh_r.at[q, d - 1], dev(zh_=plus(zh, d)))

    def spread(q):
        v = S2[q]
        for d in (1, 3, 2):
            wait(R2.at[q, d - 1], zh_r.at[q, d - 1])
            v = v + R2[q, d - 1]
        R3[q, y] = v
        for d in (1, 3, 2):
            send(R3.at[q, y], R3.at[q, y], ag_s, ag_r.at[q, d - 1], dev(y_=plus(y, d)))

    def collect(q):
        for d in (1, 3, 2):
            wait(R3.at[q, 0], ag_r.at[q, d - 1])
        return product([R3[q, j] for j in range(4)], q)

    def sib_quarter(dx):
        for dl in range(4):
            wait(sib_spot(dx, dl), sib_r.at[dx, dl])

    scale = 1.0 / tokens

    def factor_part(n):
        i = plus(y, 4 - n)

        def tile(t, _):
            at = pl.ds(pl.multiple_of(t * 128, 128), 128)
            left = AK[i, :, :, :, at].reshape(512, 128)
            right = AC[:, :, i].reshape(512, 1024)
            p = lax.dot_general(left, right, (((0,), (0,)), ((), ())), preferred_element_type=F32) * scale
            f_out[at, :] = p if n == 0 else f_out[at, :] + p
            return 0

        lax.fori_loop(0, 4, tile, 0)

    scatter()
    mine = spot(0, 0)
    for d in (1, 3, 2):
        send(mine, mine, zl_s, zl_r.at[d - 1], dev(zl_=plus(zl, d)))
    to_sib(mine, 0, 0)
    for d in (1, 3, 2):
        send(GX.at[x], GX.at[x], gx_s, gx_r.at[d - 1], dev(x_=plus(x, d)))
    to_x(mine, 0)
    for d in (1, 3, 2):
        wait(spot(0, d), zl_r.at[d - 1])
        to_x(spot(0, d), d)
        to_sib(spot(0, d), 0, d)
        if d == 1:
            for e in (1, 3, 2):
                wait(GX.at[0], gx_r.at[e - 1])
            wait(sib_spot(0, 0), sib_r.at[0, 0])
            first_partial(0)
    wait(SC, sc_r)
    over_z(1)
    over_z(3)
    for d in (1, 3, 2):
        wait(sib_spot(0, d), sib_r.at[0, d])
        first_partial(d)
    first_cross()
    over_z(0)
    for dl in (0, 1, 3, 2):
        for dx in (1, 3):
            wait(spot(dx, dl), x_r.at[dx - 1, dl])
            if (dx == 1) == (dl < 2):
                send(spot(dx, dl), spot(dx, dl), x_s, x_r.at[1, dl], dev(x_=plus(x, dx)))
            to_sib(spot(dx, dl), dx, dl)
    first_spread()
    pass_on(1)
    pass_on(3)
    relay_z()
    for dl in (0, 1, 3, 2):
        wait(spot(2, dl), x_r.at[1, dl])
        to_sib(spot(2, dl), 2, dl)
    total = first_collect(0)
    for q in (1, 3, 2):
        sib_quarter(q)
        total = total + first_collect(q)
    applied = total * scale + DAMPING * g
    APH[...] = two_terms(applied)
    for h in range(2):
        APS[h] = applied[:, 512 * h : 512 * (h + 1)]
    for q in (0, 1, 3, 2):
        partial(q)
    pass_on(0)
    pass_on(2)
    for q in (0, 1, 3, 2):
        cross(q)
    over_y(1)
    over_y(3)
    over_y(2)
    over_y(0)
    for dc in range(2):
        half = lax.rem(core + dc, 2)
        if dc == 0:
            @pl.when(diagonal)
            def _():
                pltpu.make_async_copy(APS.at[half], APT.at[core], ap_r.at[0]).start()

            @pl.when(jnp.logical_not(diagonal))
            def _():
                send(APS.at[half], APT.at[core], ap_s.at[0], ap_r.at[0], mirror[0])
        else:
            send(APS.at[half], APT.at[core], ap_s.at[1], ap_r.at[1], mirror[1])
    for q in (0, 1, 3, 2):
        spread(q)
    relay_y()
    factor_part(0)
    total = collect(0)
    for q in (1, 3, 2):
        total = total + collect(q)
    sol_out[...] = (
        3.0 * omega * g
        + (omega**3 * DAMPING - 3.0 * omega**2) * applied
        + (omega**3 / tokens) * total
    )
    for n in (1, 3, 2):
        for k in range(4):
            if n != 2 and (n == 1) == (k < 2):
                continue
            wait_y(n, k)
        factor_part(n)

    wait(APT.at[0], ap_r.at[0])
    wait(APT.at[0], ap_r.at[1])
    ap_out[...] = APT[...].reshape(32, 512)

    wait(AC.at[0:3, 0, :, 0], zl_s)
    wait(AC.at[0:3, :, :, 0], x_s)
    wait(AC.at[:, :, :, 0], sib_s)
    wait(LB.at[0, 0:7], sc_s)
    wait(LB.at[0, 0:6], zs_s.at[0])
    wait(LB.at[0:2], zs_s.at[1])
    wait(LB.at[0], v_s)
    wait(LB.at[0:3], xs_s)
    wait(AK.at[0:3], ys_s)
    wait(GX.at[0:3], gx_s)
    wait(P1.at[0:3], p1_s)
    wait(P3, p2_s)
    wait(YA.at[0:3], ya_s.at[0])
    wait(YA.at[0, 0:3], ya_s.at[1])
    wait(R1, rs_s)
    wait(R1, zh_s)
    wait(R1, ag_s)
    pl.when(jnp.logical_not(diagonal))(lambda: wait(APT.at[0], ap_s.at[0]))
    wait(APT.at[0], ap_s.at[1])


def local(acts, grads):
    tokens = 2048
    omega = step_size(16384, tokens)
    dma = pltpu.SemaphoreType.DMA
    vmem = pl.BlockSpec(memory_space=pltpu.VMEM)
    anywhere = pl.BlockSpec(memory_space=pltpu.HBM)

    def body(*refs):
        kernel(tokens, omega, *refs)

    factor, ap, sol = pl.pallas_call(
        body,
        out_shape=(
            jax.ShapeDtypeStruct((512, 1024), F32),
            jax.ShapeDtypeStruct((32, 512), F32),
            jax.ShapeDtypeStruct((16, 1024), F32),
        ),
        in_specs=[anywhere, anywhere],
        out_specs=[vmem, vmem, vmem],
        scratch_shapes=[
            pltpu.VMEM((4, 4, 4, 2, 16, 1024), BF16),
            pltpu.VMEM((4, 4, 8, 16, 512), BF16),
            pltpu.VMEM((4, 8, 16, 512), BF16),
            pltpu.VMEM((4, 2, 16, 512), BF16),
            pltpu.VMEM((16, 1024), F32),
            pltpu.VMEM((4, 32, 1024), BF16),
            pltpu.VMEM((32, 1024), BF16),
            pltpu.VMEM((4, 4, 16, 128), F32),
            pltpu.VMEM((4, 4, 16, 128), F32),
            pltpu.VMEM((4, 4, 16, 128), F32),
            pltpu.VMEM((4, 16, 128), F32),
            pltpu.VMEM((3, 4, 16, 128), F32),
            pltpu.VMEM((4, 16, 128), F32),
            pltpu.VMEM((4, 4, 16, 128), F32),
            pltpu.VMEM((4, 3, 16, 128), F32),
            pltpu.VMEM((4, 16, 128), F32),
            pltpu.VMEM((4, 3, 16, 128), F32),
            pltpu.VMEM((4, 4, 16, 128), F32),
            pltpu.VMEM((2, 16, 512), F32),
            pltpu.VMEM((2, 16, 512), F32),
            dma(()), dma(()), dma(()), dma(()), dma((3,)), dma(()), dma((3, 4)), dma(()), dma((4, 4)),
            dma((2,)), dma((4,)), dma(()), dma((4,)), dma(()), dma((3, 4)),
            dma(()), dma((3,)), dma(()), dma((4,)), dma(()), dma((3,)), dma((2,)), dma((4, 4)),
            dma(()), dma((4, 3)), dma(()), dma((4, 3)), dma(()), dma((4, 3)),
            dma((4,)), dma((2,)),
        ],
        compiler_params=pltpu.CompilerParams(
            collective_id=0, has_side_effects=True, vmem_limit_bytes=48 * 2**20
        ),
        name="everything",
    )(acts.reshape(4, 16, 1024), grads.T)
    return factor, ap.T, sol.T


def solution(mesh):
    split = Mesh(mesh.devices.reshape(4, 4, 2, 4, 4), AXES)
    return jax.shard_map(
        local,
        mesh=split,
        in_specs=(P(ROW, COL), P(COL, ROW)),
        out_specs=(P(ROW, COL), P(ROW, COL), P(COL, ROW)),
        check_vma=False,
    )
```
